32 devices in a mesh: src: 8 (over z, core), tgt: 4 (over y, x).
Axes of the slice: x: 2, y: 2, z: 4, core: 2. Of those that a mesh axis runs over, the one named last changes fastest.
Arguments:
- positions: float32 [3, 4096], P(None, ('src', 'tgt')), as said below
- contact_bodies: int32 [2, 32768], P(None, ('src', 'tgt')), may hold values from 0 to 4095, as said below
- contact_frame: float32 [9, 32768], P(None, ('src', 'tgt')), as said below
- gaps: float32 [32768], P(('src', 'tgt')), may hold values from -1 to 1
- impulse_now: float32 [32768], P(('src', 'tgt')), may hold values from 0 to 1
- impulse_prev: float32 [32768], P(('src', 'tgt')), may hold values from 0 to 1
- step_sizes: float32 [2], replicated, may hold values from 0.05 to 0.2
Outputs:
- impulse: float32 [32768], P(('src', 'tgt'))
- body_velocity: float32 [6, 4096], P(None, ('src', 'tgt'))
The draws below stay inside these ranges and needn't reach their ends.
Inputs may be any that keep to these rules, and one draw needn't show every extreme that they name: `contact_bodies`: each contact joins a body i with body i + 1, i + 32 or i + 1024, modulo 4096. `positions`: body k lies within 0.45 of the point 3 (k mod 32, k // 32 mod 32, k // 1024) along each coordinate. `contact_frame`: rows 0 to 2 of each column are a unit vector; rows 3 to 8 lie in -2 to 2.
All inputs are finite; a program needn't handle non-finite values.
Results may differ from the reference program's by a relative error of at most 0.0003.
Values sent between devices are 32-bit elements; how exact they have to be, the bound alone decides.
A program may use at most 64 MiB of HBM per device.

```python
import math
import jax
import jax.numpy as jnp
from jax import lax

ITERS = 2
BODIES = 4096
CONTACTS = 32768


def draw_positions(key, part):
    body_ids = jnp.arange(BODIES, dtype=jnp.int32)
    lattice = jnp.stack([body_ids % 32, body_ids // 32 % 32, body_ids // 1024]).astype(jnp.float32) * 3.0
    jitter = jax.random.uniform(key, (3, BODIES), jnp.float32, -0.4, 0.4)
    return lattice + jitter


def draw_contact_bodies(key, part):
    key_first, key_direction = jax.random.split(key)
    first = jax.random.randint(key_first, (CONTACTS,), 0, BODIES, jnp.int32)
    direction = jax.random.randint(key_direction, (CONTACTS,), 0, 3, jnp.int32)
    direction = direction.at[1].set(0)
    first = first.at[0].set(BODIES - 1).at[1].set(BODIES - 1)
    offset = jnp.where(direction == 0, 1, jnp.where(direction == 1, 32, 1024))
    second = (first + offset) % BODIES
    return jnp.stack([first, second]).astype(jnp.int32)


def draw_contact_frame(key, part):
    key_polar, key_azimuth, key_arms = jax.random.split(key, 3)
    polar = jax.random.uniform(key_polar, (CONTACTS,), jnp.float32, 0.0, 3.14159265)
    azimuth = jax.random.uniform(key_azimuth, (CONTACTS,), jnp.float32, -3.14159265, 3.14159265)
    normal = jnp.stack([jnp.sin(polar) * jnp.cos(azimuth), jnp.sin(polar) * jnp.sin(azimuth), jnp.cos(polar)])
    levers = jnp.clip(0.8 * jax.random.normal(key_arms, (6, CONTACTS), jnp.float32), -2.0, 2.0)
    return jnp.concatenate([normal, levers]).astype(jnp.float32)


def level_of(stream_key, extent, cuts, smallest, largest):
    level = 1.0
    for position, parts in cuts:
        draws = jax.random.uniform(jax.random.fold_in(jax.random.fold_in(stream_key, 6), position), (parts,), jnp.float32, smallest / len(cuts), largest / len(cuts))
        level = level * jnp.repeat(jnp.exp(draws), extent[position] // parts).reshape((-1,) + (1,) * (len(extent) - 1 - position))
    return level


def setup_inputs(seed: int = 0) -> dict:
    arg_keys = jax.random.split(jax.random.key(seed), 8)
    return {
        "positions": draw_positions(jax.random.fold_in(arg_keys[7], 71), 0),
        "contact_bodies": draw_contact_bodies(jax.random.fold_in(arg_keys[7], 71), 0),
        "contact_frame": draw_contact_frame(jax.random.fold_in(arg_keys[7], 71), 0),
        "gaps": jnp.clip(jax.random.uniform(arg_keys[3], (CONTACTS,), jnp.float32, -1.0, 1.0) * level_of(arg_keys[3], (CONTACTS,), ((0, 32),), -0.4, 0.0), -1.0, 1.0),
        "impulse_now": jnp.clip(1.0 * jax.random.uniform(arg_keys[4], (CONTACTS,), jnp.float32) ** level_of(arg_keys[4], (CONTACTS,), ((0, 32),), -0.2, 0.2), 0.0, 1.0),
        "impulse_prev": jnp.clip(1.0 * jax.random.uniform(arg_keys[5], (CONTACTS,), jnp.float32) ** level_of(arg_keys[5], (CONTACTS,), ((0, 32),), -0.2, 0.2), 0.0, 1.0),
        "step_sizes": jnp.clip(jax.random.uniform(arg_keys[6], (ITERS,), jnp.float32, 0.05, 0.2), 0.05, 0.2),
    }


MOMENTUM = 0.4

def cross_product(first, second):
    return jnp.stack([first[1] * second[2] - first[2] * second[1], first[2] * second[0] - first[0] * second[2], first[0] * second[1] - first[1] * second[0]])

def contact_rows(frame):
    normal = frame[0:3]
    lever_first = cross_product(frame[3:6], normal)
    lever_second = cross_product(frame[6:9], normal)
    return (jnp.concatenate([-normal, -lever_first]), jnp.concatenate([normal, lever_second]))

def pair_block(target_pos, target_ids, source_pos, source_ids, forces):
    delta_x = target_pos[0][:, None] - source_pos[0][None, :]
    delta_y = target_pos[1][:, None] - source_pos[1][None, :]
    delta_z = target_pos[2][:, None] - source_pos[2][None, :]
    coincide = target_ids[:, None] == source_ids[None, :]
    dist_sq = jnp.where(coincide, 1.0, delta_x * delta_x + delta_y * delta_y + delta_z * delta_z)
    inverse = jnp.where(coincide, 0.0, lax.rsqrt(dist_sq))
    self_term = jnp.where(coincide, 1.0, 0.0)
    unit_x = delta_x * inverse
    unit_y = delta_y * inverse
    unit_z = delta_z * inverse
    force_x, force_y, force_z = (forces[0][None, :], forces[1][None, :], forces[2][None, :])
    torque_x, torque_y, torque_z = (forces[3][None, :], forces[4][None, :], forces[5][None, :])
    inverse_sq = inverse * inverse
    c_one = 0.75 * inverse
    c_two = 0.75 * inverse_sq
    c_three = 0.375 * inverse_sq * inverse
    along_force = unit_x * force_x + unit_y * force_y + unit_z * force_z
    along_torque = unit_x * torque_x + unit_y * torque_y + unit_z * torque_z
    isotropic = c_one * (1.0 + inverse_sq * (2.0 / 3.0)) + self_term
    dyadic = c_one * (1.0 - 2.0 * inverse_sq) * along_force
    vel_x = isotropic * force_x + dyadic * unit_x + c_two * (torque_y * unit_z - torque_z * unit_y)
    vel_y = isotropic * force_y + dyadic * unit_y + c_two * (torque_z * unit_x - torque_x * unit_z)
    vel_z = isotropic * force_z + dyadic * unit_z + c_two * (torque_x * unit_y - torque_y * unit_x)
    spin_self = 0.75 * self_term - c_three
    spin_x = c_two * (force_y * unit_z - force_z * unit_y) + c_three * 3.0 * unit_x * along_torque + spin_self * torque_x
    spin_y = c_two * (force_z * unit_x - force_x * unit_z) + c_three * 3.0 * unit_y * along_torque + spin_self * torque_y
    spin_z = c_two * (force_x * unit_y - force_y * unit_x) + c_three * 3.0 * unit_z * along_torque + spin_self * torque_z
    return jnp.stack([lax.optimization_barrier(jnp.sum(vel_x, 1)), lax.optimization_barrier(jnp.sum(vel_y, 1)), lax.optimization_barrier(jnp.sum(vel_z, 1)), lax.optimization_barrier(jnp.sum(spin_x, 1)), lax.optimization_barrier(jnp.sum(spin_y, 1)), lax.optimization_barrier(jnp.sum(spin_z, 1))])

def mobility(positions, body_ids, forces):
    body_count = positions.shape[1]
    block_size = math.gcd(body_count, 256)
    blocks = body_count // block_size
    target_pos = positions.reshape(3, blocks, block_size).transpose(1, 0, 2)
    target_ids = body_ids.reshape(blocks, block_size)

    def one_block(pair):
        return pair_block(pair[0], pair[1], positions, body_ids, forces)
    result = lax.map(one_block, (target_pos, target_ids))
    return result.transpose(1, 0, 2).reshape(6, body_count)

def reference(positions, contact_bodies, contact_frame, gaps, impulse_now, impulse_prev, step_sizes):
    body_count = positions.shape[1]
    body_ids = jnp.arange(body_count, dtype=jnp.int32)
    first_rows, second_rows = contact_rows(contact_frame)
    current = impulse_now
    shifted = impulse_now + MOMENTUM * (impulse_now - impulse_prev)
    velocity = jnp.zeros((6, body_count), jnp.float32)
    for k in range(ITERS):
        forces = jnp.zeros((6, body_count), jnp.float32)
        forces = forces.at[:, contact_bodies[0]].add(first_rows * shifted[None, :])
        forces = forces.at[:, contact_bodies[1]].add(second_rows * shifted[None, :])
        velocity = mobility(positions, body_ids, forces)
        normal_rate = lax.optimization_barrier(jnp.sum(first_rows * velocity[:, contact_bodies[0]], 0)) + lax.optimization_barrier(jnp.sum(second_rows * velocity[:, contact_bodies[1]], 0))
        updated = jnp.maximum(shifted - step_sizes[k] * (gaps + normal_rate), 0.0)
        shifted = updated + MOMENTUM * (updated - current)
        current = updated
    return (current, velocity)
```

```python
import functools

import jax
import jax.numpy as jnp
from jax import lax
from jax.experimental import pallas as pl
from jax.experimental.pallas import tpu as pltpu
from jax.sharding import PartitionSpec as P

ITERS = 2
MOMENTUM = 0.4
GROUP = 16

F32 = jnp.float32
BF16 = jnp.bfloat16


def halves(value):
    high = value.astype(BF16)
    return high, (value - high.astype(F32)).astype(BF16)


def cross_rows(first, second):
    return [
        first[1] * second[2] - first[2] * second[1],
        first[2] * second[0] - first[0] * second[2],
        first[0] * second[1] - first[1] * second[0],
    ]


def kernel(
    src_count,
    tgt_count,
    pos_ref,
    bodies_ref,
    frame_ref,
    gaps_ref,
    now_ref,
    prev_ref,
    step_ref,
    impulse_ref,
    velocity_ref,
    pos_all,
    part,
    arrived,
    force_all,
    vel_all,
    target_pos,
    coef,
    total,
    spread,
    onehot,
    picked,
    send_sem,
    recv_sem,
):
    n = src_count * tgt_count
    lanes = pos_ref.shape[1]
    contacts = gaps_ref.shape[1]
    me = lax.axis_index("src") * tgt_count + lax.axis_index("tgt")

    def place(device):
        return (device // tgt_count, lax.rem(device, tgt_count))

    def send_all(source, landing, phase):
        def one(k, carry):
            device = lax.rem(me + k, n)
            pltpu.make_async_remote_copy(
                src_ref=source(device),
                dst_ref=landing.at[me],
                send_sem=send_sem.at[phase],
                recv_sem=recv_sem.at[phase],
                device_id=place(device),
                device_id_type=pl.DeviceIdType.MESH,
            ).start()
            return carry

        lax.fori_loop(1, n, one, 0)

    def wait_all(landing, sem):
        blocks = landing.at[pl.ds(0, n - 1)]
        pltpu.make_async_copy(blocks, blocks, sem).wait()

    barrier = pltpu.get_barrier_semaphore()

    def greet(k, carry):
        pl.semaphore_signal(
            barrier,
            inc=1,
            device_id=place(lax.rem(me + k, n)),
            device_id_type=pl.DeviceIdType.MESH,
        )
        return carry

    lax.fori_loop(1, n, greet, 0)

    normal = [frame_ref[r : r + 1, :] for r in range(3)]
    arm_first = [frame_ref[r : r + 1, :] for r in range(3, 6)]
    arm_second = [frame_ref[r : r + 1, :] for r in range(6, 9)]
    empty = jnp.zeros((1, contacts), F32)
    second_rows = jnp.concatenate(normal + cross_rows(arm_second, normal) + [empty, empty], 0)
    first_rows = -jnp.concatenate(normal + cross_rows(arm_first, normal) + [empty, empty], 0)
    rows = [first_rows, second_rows]

    lane_ids = lax.broadcasted_iota(jnp.int32, (lanes, contacts), 0)
    pair_half = lax.broadcasted_iota(jnp.int32, (16, contacts), 0) // 8
    block_ids = []
    for end in range(2):
        body = bodies_ref[end : end + 1, :]
        block = body // lanes
        block_ids.append(block - pair_half)
        hot = jnp.where(lane_ids == body - block * lanes, 1.0, 0.0).astype(BF16)
        onehot[0:lanes, end * contacts : (end + 1) * contacts] = hot
        onehot[lanes : 2 * lanes, end * contacts : (end + 1) * contacts] = hot

    pos_own = jnp.concatenate([pos_ref[...], jnp.zeros((5, lanes), F32)], 0)
    pos_all[me] = pos_own
    for r in range(3):
        target_pos[r] = jnp.broadcast_to(pos_own[r : r + 1, :], (lanes, lanes)).T

    pl.semaphore_wait(barrier, n - 1)
    send_all(lambda device: pos_all.at[me], pos_all, 0)

    current = now_ref[...]
    shifted = current + MOMENTUM * (current - prev_ref[...])

    for k in range(ITERS):
        pieces = []
        for end in range(2):
            value = rows[end] * shifted
            high = value.astype(BF16).astype(F32)
            low = value - high
            pieces.append(
                (jnp.concatenate([high, high], 0), jnp.concatenate([low, low], 0))
            )

        def lay_out(step, carry):
            inner = pl.multiple_of(step * 16, 16)
            for end in range(2):
                here = block_ids[end] == 2 * step
                for half in range(2):
                    spread[
                        half, pl.ds(inner, 16), end * contacts : (end + 1) * contacts
                    ] = jnp.where(here, pieces[end][half], 0.0).astype(BF16)
            return carry

        lax.fori_loop(0, n // 2, lay_out, 0)
        both = lax.dot_general(
            spread[...].reshape(2 * n * 8, 2 * contacts),
            onehot[0:lanes, :],
            (((1,), (1,)), ((), ())),
            preferred_element_type=F32,
        )
        part[k] = (both[: n * 8] + both[n * 8 :]).reshape(n, 8, lanes)
        arrived[k, me] = part[k, me]
        send_all(lambda device: part.at[k, device], arrived.at[k], 1 + 3 * k)

        if k == 0:
            wait_all(pos_all, recv_sem.at[0])

            def coefficients(step, carry):
                block = step // (lanes // GROUP)
                group = pl.ds(
                    pl.multiple_of(lax.rem(step, lanes // GROUP) * GROUP, GROUP), GROUP
                )
                dist_sq = None
                for r in range(3):
                    delta = target_pos[r, group, :] - pos_all[block, r : r + 1, :]
                    dist_sq = delta * delta if r == 0 else dist_sq + delta * delta
                inverse = lax.rsqrt(dist_sq)
                inverse_sq = inverse * inverse
                c_one = 0.75 * inverse
                gamma = c_one * inverse_sq
                scaled = gamma * inverse_sq
                coef[block, 0, group, :] = c_one + gamma * (2.0 / 3.0)
                coef[block, 1, group, :] = gamma - 2.0 * scaled
                coef[block, 2, group, :] = gamma
                coef[block, 3, group, :] = 1.5 * scaled
                return carry

            lax.fori_loop(0, n * (lanes // GROUP), coefficients, 0, unroll=2)
            diagonal = lax.broadcasted_iota(
                jnp.int32, (lanes, lanes), 0
            ) == lax.broadcasted_iota(jnp.int32, (lanes, lanes), 1)
            for c in range(4):
                coef[me, c] = jnp.where(diagonal, 0.0, coef[me, c])

        wait_all(arrived.at[k], recv_sem.at[1 + 3 * k])
        own_force = jnp.sum(arrived[k], 0)
        force_all[k, me] = own_force
        send_all(lambda device: force_all.at[k, me], force_all.at[k], 2 + 3 * k)
        wait_all(force_all.at[k], recv_sem.at[2 + 3 * k])

        def target_group(step, carry):
            group = pl.ds(pl.multiple_of(step * GROUP, GROUP), GROUP)
            where = [target_pos[r, group, :] for r in range(3)]

            def source_block(block, sums):
                x, y, z = [where[r] - pos_all[block, r : r + 1, :] for r in range(3)]
                f_x, f_y, f_z, t_x, t_y, t_z = [
                    force_all[k, block, r : r + 1, :] for r in range(6)
                ]
                alpha, beta, gamma, delta = [coef[block, c, group, :] for c in range(4)]
                along_force = beta * (x * f_x + y * f_y + z * f_z)
                along_torque = delta * (x * t_x + y * t_y + z * t_z)
                return (
                    sums[0] + (alpha * f_x + along_force * x + gamma * (t_y * z - t_z * y)),
                    sums[1] + (alpha * f_y + along_force * y + gamma * (t_z * x - t_x * z)),
                    sums[2] + (alpha * f_z + along_force * z + gamma * (t_x * y - t_y * x)),
                    sums[3] + (along_torque * x + gamma * (f_y * z - f_z * y - 0.5 * t_x)),
                    sums[4] + (along_torque * y + gamma * (f_z * x - f_x * z - 0.5 * t_y)),
                    sums[5] + (along_torque * z + gamma * (f_x * y - f_y * x - 0.5 * t_z)),
                )

            zero = jnp.zeros((GROUP, lanes), F32)
            sums = lax.fori_loop(0, n, source_block, (zero,) * 6, unroll=2)
            for r in range(6):
                total[r, group, :] = sums[r]
            return carry

        lax.fori_loop(0, lanes // GROUP, target_group, 0)
        own_velocity = jnp.concatenate(
            [jnp.sum(total[r].T, 0, keepdims=True) for r in range(6)]
            + [jnp.zeros((2, lanes), F32)],
            0,
        )
        row_ids = lax.broadcasted_iota(jnp.int32, (8, lanes), 0)
        own_velocity = own_velocity + jnp.where(row_ids < 3, 1.0, 0.75) * own_force
        vel_all[k, me] = own_velocity
        send_all(lambda device: vel_all.at[k, me], vel_all.at[k], 3 + 3 * k)
        if k == ITERS - 1:
            velocity_ref[...] = own_velocity[0:6]
        wait_all(vel_all.at[k], recv_sem.at[3 + 3 * k])

        high, low = halves(vel_all[k].reshape(n * 8, lanes))
        picked[...] = jnp.dot(
            jnp.concatenate([high, low], 1), onehot[...], preferred_element_type=F32
        )

        def pick(step, sums):
            inner = pl.multiple_of(step * 16, 16)
            return tuple(
                sums[end]
                + jnp.where(
                    block_ids[end] == 2 * step,
                    picked[pl.ds(inner, 16), end * contacts : (end + 1) * contacts],
                    0.0,
                )
                for end in range(2)
            )

        zero = jnp.zeros((16, contacts), F32)
        ends = lax.fori_loop(0, n // 2, pick, (zero, zero))
        rate = sum(rows[end] * (ends[end][0:8] + ends[end][8:16]) for end in range(2))
        normal_rate = jnp.sum(rate, 0, keepdims=True)
        updated = jnp.maximum(shifted - step_ref[k] * (gaps_ref[...] + normal_rate), 0.0)
        shifted = updated + MOMENTUM * (updated - current)
        current = updated

    impulse_ref[...] = current
    for phase in range(1 + 3 * ITERS):
        wait_all(pos_all, send_sem.at[phase])


def per_device(
    positions, contact_bodies, contact_frame, gaps, impulse_now, impulse_prev, step_sizes
):
    src_count = lax.axis_size("src")
    tgt_count = lax.axis_size("tgt")
    n = src_count * tgt_count
    lanes = positions.shape[1]
    contacts = gaps.shape[0]
    vmem = pl.BlockSpec(memory_space=pltpu.VMEM)
    impulse, velocity = pl.pallas_call(
        functools.partial(kernel, src_count, tgt_count),
        out_shape=(
            jax.ShapeDtypeStruct((1, contacts), F32),
            jax.ShapeDtypeStruct((6, lanes), F32),
        ),
        in_specs=[vmem] * 6 + [pl.BlockSpec(memory_space=pltpu.SMEM)],
        out_specs=(vmem, vmem),
        scratch_shapes=[
            pltpu.VMEM((n, 8, lanes), F32),
            pltpu.VMEM((ITERS, n, 8, lanes), F32),
            pltpu.VMEM((ITERS, n, 8, lanes), F32),
            pltpu.VMEM((ITERS, n, 8, lanes), F32),
            pltpu.VMEM((ITERS, n, 8, lanes), F32),
            pltpu.VMEM((3, lanes, lanes), F32),
            pltpu.VMEM((n, 4, lanes, lanes), F32),
            pltpu.VMEM((6, lanes, lanes), F32),
            pltpu.VMEM((2, n * 8, 2 * contacts), BF16),
            pltpu.VMEM((2 * lanes, 2 * contacts), BF16),
            pltpu.VMEM((n * 8, 2 * contacts), F32),
            pltpu.SemaphoreType.DMA((1 + 3 * ITERS,)),
            pltpu.SemaphoreType.DMA((1 + 3 * ITERS,)),
        ],
        compiler_params=pltpu.CompilerParams(
            collective_id=0, has_side_effects=True, vmem_limit_bytes=60 * 1024 * 1024
        ),
    )(
        positions,
        contact_bodies,
        contact_frame,
        gaps.reshape(1, contacts),
        impulse_now.reshape(1, contacts),
        impulse_prev.reshape(1, contacts),
        step_sizes,
    )
    return impulse.reshape(contacts), velocity


def solution(mesh):
    placed = (
        P(None, ("src", "tgt")),
        P(None, ("src", "tgt")),
        P(None, ("src", "tgt")),
        P(("src", "tgt")),
        P(("src", "tgt")),
        P(("src", "tgt")),
        P(),
    )
    return jax.shard_map(
        per_device,
        mesh=mesh,
        in_specs=placed,
        out_specs=(P(("src", "tgt")), P(None, ("src", "tgt"))),
        check_vma=False,
    )
```

```python
import functools

import jax
import jax.numpy as jnp
from jax import lax
from jax.experimental import pallas as pl
from jax.experimental.pallas import tpu as pltpu
from jax.sharding import PartitionSpec as P

ITERS = 2
MOMENTUM = 0.4
GROUP = 16

F32 = jnp.float32
BF16 = jnp.bfloat16


def halves(value):
    high = value.astype(BF16)
    return high, (value - high.astype(F32)).astype(BF16)


def cross_rows(first, second):
    return [
        first[1] * second[2] - first[2] * second[1],
        first[2] * second[0] - first[0] * second[2],
        first[0] * second[1] - first[1] * second[0],
    ]


def kernel(
    src_count,
    tgt_count,
    pos_ref,
    bodies_ref,
    frame_ref,
    gaps_ref,
    now_ref,
    prev_ref,
    step_ref,
    result_ref,
    pos_all,
    part,
    from_twin,
    summed,
    arrived,
    force_all,
    vel_all,
    target_pos,
    coef,
    total,
    spread,
    onehot,
    picked,
    send_sem,
    recv_sem,
):
    planes = src_count // 2
    chips = planes * tgt_count
    lanes = pos_ref.shape[1]
    contacts = gaps_ref.shape[1]
    src = lax.axis_index("src")
    tgt = lax.axis_index("tgt")
    core = lax.rem(src, 2)
    plane = src // 2
    me = src * tgt_count + tgt
    twin = (src + 1 - 2 * core, tgt)

    def for_peers(visit):
        def one_plane(i, carry):
            there = lax.rem(plane + i, planes)
            for j in range(tgt_count):
                visit(there, lax.rem(tgt + j, tgt_count))
            return carry

        for j in range(1, tgt_count):
            visit(plane, lax.rem(tgt + j, tgt_count))
        lax.fori_loop(1, planes, one_plane, 0)

    def start_copy(source, landing, phase, slot, device, to_twin=0):
        pltpu.make_async_remote_copy(
            src_ref=source,
            dst_ref=landing,
            send_sem=send_sem.at[phase, to_twin],
            recv_sem=recv_sem.at[phase, slot],
            device_id=device,
            device_id_type=pl.DeviceIdType.MESH,
        ).start()

    def wait_for(blocks, sem):
        pltpu.make_async_copy(blocks, blocks, sem).wait()

    def chunk(buffer, group):
        return buffer.at[pl.ds(group * tgt_count, tgt_count)]

    def gather_start(buffer, phase, height):
        block = buffer.at[me, pl.ds(0, height)]
        for_peers(
            lambda there, column: start_copy(
                block, block, phase, src, (2 * there + core, column)
            )
        )

    def gather_own(buffer, phase, height, i):
        group = 2 * lax.rem(plane + i, planes) + core
        count = tgt_count - 1 if isinstance(i, int) and i == 0 else tgt_count
        wait_for(
            buffer.at[pl.ds(group * tgt_count, count), pl.ds(0, height)],
            recv_sem.at[phase, group],
        )
        blocks = chunk(buffer, group)
        start_copy(blocks, blocks, phase, group, twin, 1)
        return group

    def gather_twin(buffer, phase, i):
        group = 2 * lax.rem(plane + i, planes) + 1 - core
        wait_for(chunk(buffer, group), recv_sem.at[phase, group])
        return group

    def gather_sent(buffer, phase, height):
        wait_for(buffer.at[pl.ds(0, chips - 1), pl.ds(0, height)], send_sem.at[phase, 0])
        wait_for(buffer.at[pl.ds(0, chips)], send_sem.at[phase, 1])

    pos_all[...] = jnp.zeros_like(pos_all)
    force_all[...] = jnp.zeros_like(force_all)
    vel_all[...] = jnp.zeros_like(vel_all)

    barrier = pltpu.get_barrier_semaphore()

    def greet(device):
        pl.semaphore_signal(
            barrier, inc=1, device_id=device, device_id_type=pl.DeviceIdType.MESH
        )

    greet(twin)
    for_peers(lambda there, column: greet((2 * there + core, column)))

    normal = [frame_ref[r : r + 1, :] for r in range(3)]
    arm_first = [frame_ref[r : r + 1, :] for r in range(3, 6)]
    arm_second = [frame_ref[r : r + 1, :] for r in range(6, 9)]
    empty = jnp.zeros((1, contacts), F32)
    second_rows = jnp.concatenate(normal + cross_rows(arm_second, normal) + [empty, empty], 0)
    first_rows = -jnp.concatenate(normal + cross_rows(arm_first, normal) + [empty, empty], 0)
    rows = [first_rows, second_rows]

    lane_ids = lax.broadcasted_iota(jnp.int32, (lanes, contacts), 0)
    pair_half = lax.broadcasted_iota(jnp.int32, (16, contacts), 0) // 8
    block_ids = []
    for end in range(2):
        body = bodies_ref[end : end + 1, :]
        block = body // lanes
        block_ids.append(block - pair_half)
        hot = jnp.where(lane_ids == body - block * lanes, 1.0, 0.0).astype(BF16)
        onehot[0:lanes, end * contacts : (end + 1) * contacts] = hot
        onehot[lanes : 2 * lanes, end * contacts : (end + 1) * contacts] = hot

    pos_own = jnp.concatenate([pos_ref[...], jnp.zeros((5, lanes), F32)], 0)
    pos_all[me] = pos_own
    for r in range(3):
        target_pos[r] = jnp.broadcast_to(pos_own[r : r + 1, :], (lanes, lanes)).T

    pl.semaphore_wait(barrier, chips)
    gather_start(pos_all, 0, 3)

    current = now_ref[...]
    shifted = current + MOMENTUM * (current - prev_ref[...])

    def first_block(step, parity):
        per_plane = tgt_count // 2
        there = step // per_plane
        return (2 * there + parity) * tgt_count + 2 * lax.rem(step, per_plane)

    for k in range(ITERS):
        phase_sum, phase_force, phase_vel = 1 + 3 * k, 2 + 3 * k, 3 + 3 * k

        pieces = []
        for end in range(2):
            value = rows[end] * shifted
            high = value.astype(BF16).astype(F32)
            low = value - high
            pieces.append(
                (jnp.concatenate([high, high], 0), jnp.concatenate([low, low], 0))
            )

        def scatter(parity):
            def lay_out(step, carry):
                inner = pl.multiple_of(step * 16, 16)
                for end in range(2):
                    here = block_ids[end] == first_block(step, parity)
                    for half in range(2):
                        spread[
                            half, pl.ds(inner, 16), end * contacts : (end + 1) * contacts
                        ] = jnp.where(here, pieces[end][half], 0.0).astype(BF16)
                return carry

            lax.fori_loop(0, chips // 2, lay_out, 0)
            both = lax.dot_general(
                spread[...].reshape(2 * chips * 8, 2 * contacts),
                onehot[0:lanes, :],
                (((1,), (1,)), ((), ())),
                preferred_element_type=F32,
            )
            return (both[: chips * 8] + both[chips * 8 :]).reshape(chips, 8, lanes)

        part[k] = scatter(1 - core)
        start_copy(part.at[k], from_twin.at[k], phase_sum, 0, twin, 1)
        if k == 0:
            gather_own(pos_all, 0, 3, 0)

            def pass_on(i, carry):
                gather_own(pos_all, 0, 3, i)
                return carry

            lax.fori_loop(1, planes, pass_on, 0)
        mine = scatter(core)
        wait_for(from_twin.at[k], recv_sem.at[phase_sum, 0])
        summed[k] = mine + from_twin[k]
        chip = plane * tgt_count + tgt
        for_peers(
            lambda there, column: start_copy(
                summed.at[k, there * tgt_count + column, pl.ds(0, 6)],
                arrived.at[k, chip, pl.ds(0, 6)],
                phase_sum,
                1,
                (2 * there + core, column),
            )
        )
        arrived[k, chip] = summed[k, chip]

        if k == 0:
            def from_the_twin(i, carry):
                gather_twin(pos_all, 0, i)
                return carry

            lax.fori_loop(0, planes, from_the_twin, 0)

            def coefficients(step, carry):
                block = step // (lanes // GROUP)
                group = pl.ds(
                    pl.multiple_of(lax.rem(step, lanes // GROUP) * GROUP, GROUP), GROUP
                )
                dist_sq = None
                for r in range(3):
                    delta = target_pos[r, group, :] - pos_all[block, r : r + 1, :]
                    dist_sq = delta * delta if r == 0 else dist_sq + delta * delta
                inverse = lax.rsqrt(dist_sq)
                inverse_sq = inverse * inverse
                c_one = 0.75 * inverse
                gamma = c_one * inverse_sq
                scaled = gamma * inverse_sq
                coef[block, 0, group, :] = c_one + gamma * (2.0 / 3.0)
                coef[block, 1, group, :] = gamma - 2.0 * scaled
                coef[block, 2, group, :] = gamma
                coef[block, 3, group, :] = 1.5 * scaled
                return carry

            lax.fori_loop(0, 2 * chips * (lanes // GROUP), coefficients, 0, unroll=2)
            diagonal = lax.broadcasted_iota(
                jnp.int32, (lanes, lanes), 0
            ) == lax.broadcasted_iota(jnp.int32, (lanes, lanes), 1)
            for c in range(4):
                coef[me, c] = jnp.where(diagonal, 0.0, coef[me, c])

        wait_for(
            arrived.at[k, pl.ds(0, chips - 1), pl.ds(0, 6)], recv_sem.at[phase_sum, 1]
        )
        own_force = jnp.sum(arrived[k, :, 0:6], 0)
        force_all[k, me, 0:6] = own_force
        forces = force_all.at[k]
        gather_start(forces, phase_force, 6)

        def add_pairs(chunk_id, first):
            def target_group(step, carry):
                group = pl.ds(pl.multiple_of(step * GROUP, GROUP), GROUP)
                where = [target_pos[r, group, :] for r in range(3)]
                if first:
                    sums = [jnp.zeros((GROUP, lanes), F32)] * 6
                else:
                    sums = [total[r, group, :] for r in range(6)]
                for j in range(tgt_count):
                    block = chunk_id * tgt_count + j
                    x, y, z = [where[r] - pos_all[block, r : r + 1, :] for r in range(3)]
                    f_x, f_y, f_z, t_x, t_y, t_z = [
                        force_all[k, block, r : r + 1, :] for r in range(6)
                    ]
                    alpha, beta, gamma, delta = [coef[block, c, group, :] for c in range(4)]
                    along_force = beta * (x * f_x + y * f_y + z * f_z)
                    along_torque = delta * (x * t_x + y * t_y + z * t_z)
                    sums = [
                        sums[0] + (alpha * f_x + along_force * x + gamma * (t_y * z - t_z * y)),
                        sums[1] + (alpha * f_y + along_force * y + gamma * (t_z * x - t_x * z)),
                        sums[2] + (alpha * f_z + along_force * z + gamma * (t_x * y - t_y * x)),
                        sums[3] + (along_torque * x + gamma * (f_y * z - f_z * y - 0.5 * t_x)),
                        sums[4] + (along_torque * y + gamma * (f_z * x - f_x * z - 0.5 * t_y)),
                        sums[5] + (along_torque * z + gamma * (f_x * y - f_y * x - 0.5 * t_z)),
                    ]
                for r in range(6):
                    total[r, group, :] = sums[r]
                return carry

            lax.fori_loop(0, lanes // GROUP, target_group, 0)

        add_pairs(gather_own(forces, phase_force, 6, 0), True)

        def peers_chunk(i, carry):
            add_pairs(gather_own(forces, phase_force, 6, i), False)
            return carry

        def twins_chunk(i, carry):
            add_pairs(gather_twin(forces, phase_force, i), False)
            return carry

        lax.fori_loop(1, planes, peers_chunk, 0)
        lax.fori_loop(0, planes, twins_chunk, 0)

        own_velocity = jnp.concatenate(
            [jnp.sum(total[r].T, 0, keepdims=True) for r in range(6)], 0
        )
        row_ids = lax.broadcasted_iota(jnp.int32, (6, lanes), 0)
        own_velocity = own_velocity + jnp.where(row_ids < 3, 1.0, 0.75) * own_force
        vel_all[k, me, 0:6] = own_velocity
        velocities = vel_all.at[k]
        gather_start(velocities, phase_vel, 6)

        def pick_half(parity, ends):
            blocks = [
                vel_all[k, pl.ds((2 * p + parity) * tgt_count, tgt_count)]
                for p in range(planes)
            ]
            high, low = halves(jnp.concatenate(blocks, 0).reshape(chips * 8, lanes))
            picked[...] = jnp.dot(
                jnp.concatenate([high, low], 1), onehot[...], preferred_element_type=F32
            )

            def pick(step, sums):
                inner = pl.multiple_of(step * 16, 16)
                return tuple(
                    sums[end]
                    + jnp.where(
                        block_ids[end] == first_block(step, parity),
                        picked[pl.ds(inner, 16), end * contacts : (end + 1) * contacts],
                        0.0,
                    )
                    for end in range(2)
                )

            return lax.fori_loop(0, chips // 2, pick, ends)

        gather_own(velocities, phase_vel, 6, 0)

        def pass_velocity(i, carry):
            gather_own(velocities, phase_vel, 6, i)
            return carry

        def take_velocity(i, carry):
            gather_twin(velocities, phase_vel, i)
            return carry

        lax.fori_loop(1, planes, pass_velocity, 0)
        zero = jnp.zeros((16, contacts), F32)
        ends = pick_half(core, (zero, zero))
        lax.fori_loop(0, planes, take_velocity, 0)
        ends = pick_half(1 - core, ends)
        rate = sum(rows[end] * (ends[end][0:8] + ends[end][8:16]) for end in range(2))
        normal_rate = jnp.sum(rate, 0, keepdims=True)
        updated = jnp.maximum(shifted - step_ref[k] * (gaps_ref[...] + normal_rate), 0.0)
        shifted = updated + MOMENTUM * (updated - current)
        current = updated

    result_ref[0:6, :] = own_velocity
    result_ref[6:8, :] = jnp.zeros((2, lanes), F32)
    result_ref[8:, :] = current.reshape(contacts // lanes, lanes)

    gather_sent(pos_all, 0, 3)
    for k in range(ITERS):
        wait_for(part.at[k], send_sem.at[1 + 3 * k, 1])
        wait_for(arrived.at[k, pl.ds(0, chips - 1), pl.ds(0, 6)], send_sem.at[1 + 3 * k, 0])
        gather_sent(force_all.at[k], 2 + 3 * k, 6)
        gather_sent(vel_all.at[k], 3 + 3 * k, 6)


def per_device(
    positions, contact_bodies, contact_frame, gaps, impulse_now, impulse_prev, step_sizes
):
    src_count = lax.axis_size("src")
    tgt_count = lax.axis_size("tgt")
    n = src_count * tgt_count
    lanes = positions.shape[1]
    contacts = gaps.shape[0]
    vmem = pl.BlockSpec(memory_space=pltpu.VMEM)
    result = pl.pallas_call(
        functools.partial(kernel, src_count, tgt_count),
        out_shape=jax.ShapeDtypeStruct((8 + contacts // lanes, lanes), F32),
        in_specs=[vmem] * 6 + [pl.BlockSpec(memory_space=pltpu.SMEM)],
        out_specs=vmem,
        scratch_shapes=[
            pltpu.VMEM((n, 8, lanes), F32),
            pltpu.VMEM((ITERS, n // 2, 8, lanes), F32),
            pltpu.VMEM((ITERS, n // 2, 8, lanes), F32),
            pltpu.VMEM((ITERS, n // 2, 8, lanes), F32),
            pltpu.VMEM((ITERS, n // 2, 8, lanes), F32),
            pltpu.VMEM((ITERS, n, 8, lanes), F32),
            pltpu.VMEM((ITERS, n, 8, lanes), F32),
            pltpu.VMEM((3, lanes, lanes), F32),
            pltpu.VMEM((n, 4, lanes, lanes), F32),
            pltpu.VMEM((6, lanes, lanes), F32),
            pltpu.VMEM((2, n * 4, 2 * contacts), BF16),
            pltpu.VMEM((2 * lanes, 2 * contacts), BF16),
            pltpu.VMEM((n * 4, 2 * contacts), F32),
            pltpu.SemaphoreType.DMA((1 + 3 * ITERS, 2)),
            pltpu.SemaphoreType.DMA((1 + 3 * ITERS, src_count)),
        ],
        compiler_params=pltpu.CompilerParams(
            collective_id=0, has_side_effects=True, vmem_limit_bytes=60 * 1024 * 1024
        ),
    )(
        positions,
        contact_bodies,
        contact_frame,
        gaps.reshape(1, contacts),
        impulse_now.reshape(1, contacts),
        impulse_prev.reshape(1, contacts),
        step_sizes,
    )
    return result[8:].reshape(contacts), result[0:6]


def solution(mesh):
    placed = (
        P(None, ("src", "tgt")),
        P(None, ("src", "tgt")),
        P(None, ("src", "tgt")),
        P(("src", "tgt")),
        P(("src", "tgt")),
        P(("src", "tgt")),
        P(),
    )
    return jax.shard_map(
        per_device,
        mesh=mesh,
        in_specs=placed,
        out_specs=(P(("src", "tgt")), P(None, ("src", "tgt"))),
        check_vma=False,
    )
```
